256 devices in a mesh: ta: 16 (over y, x), ha: 8 (over z_hi, core), hd: 2 (over z_lo).
Axes of the slice: x: 4, y: 4, z: 8 (z_hi: 4, z_lo: 2; z = z_hi * 2 + z_lo), core: 2. Of those that a mesh axis runs over, the one named last changes fastest.
Arguments:
- query: bfloat16 [32, 32, 64, 1536], P('ta', 'ha', None, 'hd'), may hold values from -6 to 6
- keys: bfloat16 [32, 32, 64, 1536], P('ta', 'ha', None, 'hd'), may hold values from -6 to 6
- values: bfloat16 [32, 32, 64, 1536], P('ta', 'ha', None, 'hd'), may hold values from -6 to 6
- selected: int32 [16, 8, 4, 4], P('ta', 'ha'), may hold values from 0 to 15, all different within a row; in each aligned block of 4 rows (0 to 3, 4 to 7, ..., all dimensions but the last counted through in order) at most 2 rows name the same one
- window_mask: int32 [16, 8, 4, 27], P('ta', 'ha'), may hold values 0 or 1
Outputs:
- attended: bfloat16 [32, 32, 64, 1536], P('ta', 'ha', None, 'hd')
The draws below stay inside these ranges and needn't reach their ends.
Inputs may be any that keep to these rules, and one draw needn't show every extreme that they name: `selected`: each query tile names 4 different time shards; among the 4 query tiles of one shard no time shard is named more than 2 times, and in every draw some shard names one exactly 2 times. `window_mask`: entry 13 (the tile itself) is not read.
All inputs are finite; a program needn't handle non-finite values. No bound on the sum of `window_mask` on one device may be relied on, other than what follows from the above.
Results may differ from the reference program's by a relative error of at most 0.011.
Values may be sent and summed in bfloat16 or wider, within the bound.
No kernel may reach another device: no remote copies, remote signals or barrier semaphores. Data moves between devices by JAX's collectives and lax.ppermute only.
A program may use at most 128 MiB of HBM per device.

```python
import math
import jax
import jax.numpy as jnp
import numpy as np
from jax import lax

HEAD_DIM = 128
FRAMES_DEV = 2
ROWS_DEV = 4
COLS = 64
TILE_H = 4
TILE_W = 32
SEL = 4
QT = 4
MOST = 2
CHANNELS = 1536
FRAMES = 32
ROWS = 32
N_TA = 16
N_HA = 8


def draw_query(key, part):
    seeded = jax.random.fold_in(key, 11)
    drawn = jnp.clip(jax.random.normal(seeded, (FRAMES, ROWS, COLS, CHANNELS), jnp.float32), -6.0, 6.0)
    return drawn.astype(jnp.bfloat16)


def draw_keys(key, part):
    seeded = jax.random.fold_in(key, 12)
    drawn = jnp.clip(jax.random.normal(seeded, (FRAMES, ROWS, COLS, CHANNELS), jnp.float32), -6.0, 6.0)
    return drawn.astype(jnp.bfloat16)


def touch_ends(values, stream_key, least, high):
    spot = [jax.random.randint(jax.random.fold_in(stream_key, axis), (), 0, length) for axis, length in enumerate(values.shape)]
    main_axis = values.shape.index(max(values.shape))
    neighbour = spot[:main_axis] + [(spot[main_axis] + 1) % values.shape[main_axis]] + spot[main_axis + 1:]
    return values.at[tuple(spot)].set(least).at[tuple(neighbour)].set(high)


def block_scale(stream_key, dims, shards, low, high):
    def one(dim, shards_of):
        draws = jax.random.uniform(jax.random.fold_in(jax.random.fold_in(stream_key, 6), dim), (shards_of,), jnp.float32, low / len(shards), high / len(shards))
        return jnp.repeat(jnp.exp(draws), dims[dim] // shards_of).reshape((-1,) + (1,) * (len(dims) - dim - 1))

    gain = one(*shards[0])
    for cut in shards[1:]:
        gain = gain * one(*cut)
    return gain


def deal_out(own_key, own, number, rows, amount, top, limit, skew):
    sequence = jax.random.permutation(own_key, amount)
    packed, usual = portions_of(amount, rows * top, limit, skew, True), portions_of(amount, rows * top, limit, skew, False)
    places = jnp.arange(amount)

    def named(sizes, offset_by):
        used = int((sizes > 0).sum())
        fixed = max(1, used // 4)
        moved = fixed + (places - fixed + offset_by * (used - fixed)) % max(1, amount - fixed)
        return jnp.zeros((amount,), jnp.int32).at[sequence[jnp.where(places < fixed, places, moved)]].set(jnp.asarray(sizes, jnp.int32))

    sizes = jnp.where(number % 4 == 0, named(packed, number // 4), named(usual, number - number // 4 - 1))
    mixed = jax.random.permutation(jax.random.fold_in(own, 3), amount)
    donor, taker = mixed[0:amount // 2 * 2:2], mixed[1:amount // 2 * 2:2]
    margin = jnp.minimum(sizes[donor] - 1, limit - sizes[taker]) // 2
    margin = jnp.where((donor == sequence[0]) | (taker == sequence[0]) | (sizes[taker] == 0), 0, jnp.maximum(margin, 0))
    moved = jax.random.randint(jax.random.fold_in(own, 4), (amount // 2,), 0, 1 << 20) % (margin + 1)
    sizes = sizes.at[donor].add(-moved).at[taker].add(moved)
    items = jnp.searchsorted(jnp.cumsum(sizes), jnp.arange(rows * top), side="right").astype(jnp.int32)
    table = items.reshape(top, rows).T
    table = table[jax.random.permutation(jax.random.fold_in(own, 1), rows)]
    offset_by = jax.random.randint(jax.random.fold_in(own, 2), (rows, 1), 0, top)
    return jnp.take_along_axis(table, (jnp.arange(top)[None, :] + offset_by) % top, axis=1)


def portions_of(number_of, total, reach, lean, full):
    portions = [(1 << 20) // math.isqrt(grade ** lean) + 1 for grade in range(1, number_of + 1)]
    largest = reach if full else min(reach, max(-(-total // number_of), total * portions[0] // sum(portions)))
    least = 1 if total - largest >= number_of - 1 else 0
    counts, surplus = [largest] + [least] * (number_of - 1), total - largest - least * (number_of - 1)
    while surplus > 0:
        free = [i for i in range(1, number_of) if counts[i] < largest] or [i for i in range(1, number_of) if counts[i] < reach]
        pool, budget = sum([portions[i] for i in free]), surplus
        for i in free:
            addition = min(reach - counts[i], max(1, budget * portions[i] // pool), surplus)
            counts[i] = counts[i] + addition
            surplus = surplus - addition
    return np.array(counts)


def centred(rng, extent, spread, most, cuts=(), kind=jnp.bfloat16):
    entries = jax.random.normal(rng, extent, jnp.float32) * spread
    if len(cuts) > 0:
        entries = block_scale(rng, extent, cuts, -0.22, 0.18) * entries
    return jnp.clip(entries, min=-most, max=most).astype(kind)


def setup_inputs(seed: int = 0) -> dict:
    splits = jax.random.split(jax.random.key(seed), 6)
    query = draw_query(jax.random.fold_in(splits[5], 71), 0)
    keys = draw_keys(jax.random.fold_in(splits[5], 71), 0)
    values = centred(splits[2], (FRAMES, ROWS, COLS, CHANNELS), 1.0, 6.0, ((0, 16), (1, 8), (3, 2)))
    selected_keys = jax.random.split(jax.random.fold_in(splits[3], 1), N_TA * N_HA * QT // QT)
    selected_turns = jax.random.permutation(jax.random.fold_in(splits[3], 3), N_TA * N_HA * QT // QT)
    selected = jax.vmap(lambda own, number: deal_out(jax.random.fold_in(splits[3], 2), own, number, QT, N_TA, SEL, MOST, 1))(selected_keys, selected_turns).reshape((N_TA, N_HA, QT, SEL))
    window_mask = touch_ends((jax.random.randint(splits[4], (N_TA, N_HA, QT, 27), 0, 2) < 1).astype(jnp.int32), jax.random.fold_in(splits[4], 1), 0, 1)
    return {"query": query, "keys": keys, "values": values, "selected": selected, "window_mask": window_mask}


def attend(query_tile, key_rows, value_rows, usable):
    head_count = query_tile.shape[-1] // HEAD_DIM
    query_heads = query_tile.reshape(-1, head_count, HEAD_DIM).astype(jnp.float32)
    key_heads = key_rows.reshape(-1, head_count, HEAD_DIM).astype(jnp.float32)
    value_heads = value_rows.reshape(-1, head_count, HEAD_DIM).astype(jnp.float32)
    scores = jnp.einsum("qhd,khd->hqk", query_heads, key_heads) * (HEAD_DIM ** -0.5)
    scores = jnp.where(usable[None, None, :], scores, -jnp.inf)
    highest = jnp.max(scores, axis=-1, keepdims=True)
    raised = jnp.exp(scores - highest)
    totals = jnp.sum(raised, axis=-1, keepdims=True)
    weights = (raised / totals).astype(jnp.bfloat16)
    mixed = jnp.einsum("hqk,khd->qhd", weights.astype(jnp.float32), value_heads)
    return mixed.reshape(-1, head_count * HEAD_DIM).astype(jnp.bfloat16)


def reference(query, keys, values, selected, window_mask):
    row_tiles = ROWS // TILE_H
    col_tiles = COLS // TILE_W
    shard_tiles = ROWS_DEV // TILE_H

    def to_grid(tables, breadth):
        tables = tables.reshape(N_TA, N_HA, FRAMES_DEV, shard_tiles, col_tiles, breadth)
        return tables.transpose(0, 2, 1, 3, 4, 5).reshape(FRAMES, row_tiles, col_tiles, breadth)

    chosen = to_grid(selected, SEL)
    window_marks = to_grid(window_mask, 27)
    margins = ((1, 1), (TILE_H, TILE_H), (TILE_W, TILE_W), (0, 0))
    key_pad = jnp.pad(keys, margins)
    value_pad = jnp.pad(values, margins)
    step_time = jnp.asarray(np.repeat([-1, 0, 1], 9), jnp.int32)
    step_rows = jnp.asarray(np.tile(np.repeat([-1, 0, 1], 3), 3), jnp.int32)
    step_cols = jnp.asarray(np.tile([-1, 0, 1], 9), jnp.int32)
    tile_size = TILE_H * TILE_W
    zero = jnp.zeros((), jnp.int32)

    def one_tile(number):
        number = number.astype(jnp.int32)
        frame_at = (number // (row_tiles * col_tiles)).astype(jnp.int32)
        row_tile = ((number // col_tiles) % row_tiles).astype(jnp.int32)
        col_tile = (number % col_tiles).astype(jnp.int32)
        row_start = (row_tile * TILE_H).astype(jnp.int32)
        col_start = (col_tile * TILE_W).astype(jnp.int32)
        query_tile = lax.dynamic_slice(query, (frame_at, row_start, col_start, zero), (1, TILE_H, TILE_W, CHANNELS)).reshape(tile_size, CHANNELS)

        def window(padded):
            region = lax.dynamic_slice(padded, (frame_at, row_start, col_start, zero), (3, 3 * TILE_H, 3 * TILE_W, CHANNELS))
            region = region.reshape(3, 3, TILE_H, 3, TILE_W, CHANNELS).transpose(0, 1, 3, 2, 4, 5)
            return region.reshape(27 * tile_size, CHANNELS)

        def distant(source_array):
            pieces = []
            for position in range(SEL):
                source = (chosen[frame_at, row_tile, col_tile, position] * FRAMES_DEV + frame_at % FRAMES_DEV).astype(jnp.int32)
                piece = lax.dynamic_slice(source_array, (source, row_start, col_start, zero), (1, TILE_H, TILE_W, CHANNELS))
                pieces.append(piece.reshape(tile_size, CHANNELS))
            return jnp.concatenate(pieces, 0)

        frame_near = frame_at + step_time
        row_near = row_tile + step_rows
        col_near = col_tile + step_cols
        inside = (frame_near >= 0) & (frame_near < FRAMES) & (row_near >= 0) & (row_near < row_tiles) & (col_near >= 0) & (col_near < col_tiles)
        switched = inside & ((window_marks[frame_at, row_tile, col_tile] == 1) | (jnp.arange(27, dtype=jnp.int32) == 13))
        usable = jnp.concatenate([jnp.repeat(switched, tile_size), jnp.ones((SEL * tile_size,), jnp.bool_)])
        key_rows = jnp.concatenate([window(key_pad), distant(keys)], 0)
        value_rows = jnp.concatenate([window(value_pad), distant(values)], 0)
        return attend(query_tile, key_rows, value_rows, usable)

    tile_numbers = jnp.arange(FRAMES * row_tiles * col_tiles, dtype=jnp.int32).reshape(-1, 16)
    attended = lax.map(jax.vmap(one_tile), tile_numbers)
    attended = attended.reshape(FRAMES, row_tiles, col_tiles, TILE_H, TILE_W, CHANNELS).transpose(0, 1, 3, 2, 4, 5)
    return attended.reshape(FRAMES, ROWS, COLS, CHANNELS)
```

```python
import functools
import jax
import jax.numpy as jnp
import numpy as np
from jax import lax
from jax.experimental import pallas as pl
from jax.experimental.pallas import tpu as pltpu
from jax.sharding import PartitionSpec as P

HEAD = 128
TILE = 128
SEL = 4
SIDE = 4
TA = SIDE * SIDE
HA = 8
META = 128
ROWS = 512
STAT = 32
NONE = -1e30
SCALE = float(HEAD ** -0.5)
LOG2E = float(np.log2(np.e))
VMEM_LIMIT = 50 * 1024 * 1024


def along_x(step):
    return [(SIDE * y + x, SIDE * y + (x + step) % SIDE) for y in range(SIDE) for x in range(SIDE)]


def along_y(step):
    return [(SIDE * y + x, SIDE * ((y + step) % SIDE) + x) for y in range(SIDE) for x in range(SIDE)]


def attend_tile(heads, tile, count, listed, q_ref, k_ref, v_ref, o_ref, s_ref, m_ref, l_ref, a_ref):
    frame, col = tile // 2, tile % 2
    lanes = [pl.ds(h * HEAD, HEAD) for h in range(heads)]

    def rows(r):
        return pl.ds(pl.multiple_of(frame * 256 + r * 64 + col * 32, 32), 32)

    stat_lanes = pl.ds(pl.multiple_of(tile * TILE, TILE), TILE)

    @pl.when(count == 0)
    def _():
        for r in range(4):
            o_ref[rows(r), :] = jnp.zeros((32, heads * HEAD), jnp.bfloat16)
        value = jnp.full((16, TILE), NONE, jnp.float32).astype(jnp.bfloat16)
        first = lax.broadcasted_iota(jnp.int32, (16, TILE), 0) < 8
        o_ref[pl.ds(ROWS, 16), stat_lanes] = jnp.where(first, value, jnp.zeros_like(value))
        o_ref[pl.ds(ROWS + 16, 16), stat_lanes] = jnp.zeros((16, TILE), jnp.bfloat16)

    @pl.when(count > 0)
    def _():
        for h in range(heads):
            m_ref[h] = jnp.full((TILE, TILE), NONE, jnp.float32)
            l_ref[h] = jnp.zeros((TILE, TILE), jnp.float32)
            a_ref[h] = jnp.zeros((TILE, HEAD), jnp.float32)

        def first_pass(j, carry):
            at = listed[j]
            for h in range(heads):
                q = q_ref[frame, :, col, :, lanes[h]].reshape(TILE, HEAD)
                k = k_ref[at // 2, :, at % 2, :, lanes[h]].reshape(TILE, HEAD)
                s = lax.dot_general(q, k, (((1,), (1,)), ((), ())), preferred_element_type=jnp.float32)
                s_ref[j, h] = s
                m_ref[h] = jnp.maximum(m_ref[h], s)
            return carry

        lax.fori_loop(0, count, first_pass, 0)
        for h in range(heads):
            m_ref[h] = jnp.broadcast_to(jnp.max(m_ref[h], axis=1, keepdims=True), (TILE, TILE))

        def second_pass(j, carry):
            at = listed[j]
            for h in range(heads):
                v = v_ref[at // 2, :, at % 2, :, lanes[h]].reshape(TILE, HEAD)
                p = jnp.exp2((s_ref[j, h] - m_ref[h]) * (SCALE * LOG2E))
                l_ref[h] += p
                a_ref[h] += jnp.dot(p.astype(jnp.bfloat16), v, preferred_element_type=jnp.float32)
            return carry

        lax.fori_loop(0, count, second_pass, 0)
        lane = lax.broadcasted_iota(jnp.int32, (TILE, TILE), 1)
        stats = jnp.zeros((TILE, TILE), jnp.float32)
        for h in range(heads):
            total = jnp.sum(l_ref[h], axis=1, keepdims=True)
            out = (a_ref[h] * (1.0 / total)).astype(jnp.bfloat16)
            for r in range(4):
                o_ref[rows(r), lanes[h]] = out[r * 32:(r + 1) * 32]
            stats = jnp.where(lane == h, m_ref[h] * SCALE + jnp.log(total), stats)
        turned = stats.T[0:8]
        high = turned.astype(jnp.bfloat16).astype(jnp.float32)
        mid = (turned - high).astype(jnp.bfloat16).astype(jnp.float32)
        low = turned - high - mid
        o_ref[pl.ds(ROWS, 16), stat_lanes] = jnp.concatenate([high, mid], 0).astype(jnp.bfloat16)
        o_ref[pl.ds(ROWS + 16, 16), stat_lanes] = jnp.concatenate([low, low], 0).astype(jnp.bfloat16)


def window_kernel(heads, place, meta, q0, q1, q2, k0, kr, kl, ke, v0, vr, vl, ve, o0, o1, o2,
                  qb0, qb1, qb2, kb, vb, listed, s_ref, m_ref, l_ref, a_ref, sems):
    tx, ty, height = place[0], place[1], place[2]
    shard = ty * SIDE + tx
    copies = []

    def copy(src, dst, n):
        c = pltpu.make_async_copy(src, dst, sems.at[n])
        c.start()
        copies.append(c)

    for n, (src, dst) in enumerate(((q0, qb0), (q1, qb1), (q2, qb2))):
        copy(src, dst, n)
    for n, (own, left, right, edge, dst) in enumerate(((k0, kr, kl, ke, kb), (v0, vr, vl, ve, vb))):
        copy(own, dst.at[pl.ds(1, 2)], 3 + 3 * n)

        @pl.when(tx == 0)
        def _():
            pltpu.make_async_copy(edge, dst.at[pl.ds(0, 1)], sems.at[4 + 3 * n]).start()

        @pl.when(tx != 0)
        def _():
            pltpu.make_async_copy(left.at[pl.ds(1, 1)], dst.at[pl.ds(0, 1)], sems.at[4 + 3 * n]).start()

        @pl.when(tx == SIDE - 1)
        def _():
            pltpu.make_async_copy(edge, dst.at[pl.ds(3, 1)], sems.at[5 + 3 * n]).start()

        @pl.when(tx != SIDE - 1)
        def _():
            pltpu.make_async_copy(right.at[pl.ds(0, 1)], dst.at[pl.ds(3, 1)], sems.at[5 + 3 * n]).start()

        copies.append(pltpu.make_async_copy(edge, dst.at[pl.ds(0, 1)], sems.at[4 + 3 * n]))
        copies.append(pltpu.make_async_copy(edge, dst.at[pl.ds(3, 1)], sems.at[5 + 3 * n]))
    for c in copies:
        c.wait()

    for dh, qb, o_ref in ((0, qb0, o0), (1, qb1, o1), (-1, qb2, o2)):
        asker = height - dh
        there = (asker >= 0) & (asker < HA)
        base = (shard * HA + jnp.clip(asker, 0, HA - 1)) * META + TA

        def one_tile(tile, carry):
            frame, col = tile // 2, tile % 2
            count = jnp.int32(0)
            for df in range(3):
                near = 2 * shard + frame + df - 1
                inside = there & (near >= 0) & (near < 2 * TA)
                for kw in range(2):
                    number = df * 9 + (dh + 1) * 3 + (kw - col + 1)
                    used = (meta[base + tile * 27 + number] == 1) | ((dh == 0) & (number == 13))
                    listed[count] = (frame + df) * 2 + kw
                    count = count + (used & inside).astype(jnp.int32)
            attend_tile(heads, tile, count, listed, qb, kb, vb, o_ref, s_ref, m_ref, l_ref, a_ref)
            return carry

        lax.fori_loop(0, 4, one_tile, 0)


def far_kernel(heads, place, meta, q0, q1, q2, q3, k0, k1, k2, k3, v0, v1, v2, v3, o0, o1, o2, o3,
               qb0, qb1, qb2, qb3, kb, vb, listed, s_ref, m_ref, l_ref, a_ref, sems):
    tx, ty, height = place[0], place[1], place[2]
    copies = []
    for src, dst in ((q0, qb0), (q1, qb1), (q2, qb2), (q3, qb3)):
        copies.append((src, dst))
    for n, (a, b) in enumerate(((k0, v0), (k1, v1), (k2, v2), (k3, v3))):
        copies.append((a, kb.at[pl.ds(2 * n, 2)]))
        copies.append((b, vb.at[pl.ds(2 * n, 2)]))
    copies = [pltpu.make_async_copy(src, dst, sems.at[n]) for n, (src, dst) in enumerate(copies)]
    for c in copies:
        c.start()
    for c in copies:
        c.wait()

    for back, qb, o_ref in ((0, qb0, o0), (1, qb1, o1), (2, qb2, o2), (3, qb3, o3)):
        asker = lax.rem(ty + SIDE - back, SIDE) * SIDE + tx
        base = (asker * HA + height) * META

        def one_tile(tile, carry):
            count = jnp.int32(0)
            for j in range(SEL):
                owner = meta[base + tile * SEL + j]
                piece = lax.rem(owner + SIDE - tx, SIDE)
                listed[count] = (piece * 2 + tile // 2) * 2 + tile % 2
                count = count + (owner // SIDE == ty).astype(jnp.int32)
            attend_tile(heads, tile, count, listed, qb, kb, vb, o_ref, s_ref, m_ref, l_ref, a_ref)
            return carry

        lax.fori_loop(0, 4, one_tile, 0)


def combine_kernel(heads, parts, place, *refs):
    tokens, stats, out = refs[:parts], refs[parts:2 * parts], refs[2 * parts]
    frame = pl.program_id(0)
    height = place[2]
    there = {5: height > 0, 6: height < HA - 1}
    for col in range(2):
        at = pl.ds(pl.multiple_of((frame * 2 + col) * TILE, TILE), TILE)
        logs = []
        for n in range(parts):
            s = stats[n][:, at].astype(jnp.float32)
            log = s[0:8] + s[8:16] + s[16:24]
            if n in there:
                log = jnp.where(there[n], log, NONE)
            logs.append(log)
        top = functools.reduce(jnp.maximum, logs)
        raised = [jnp.exp2((log - top) * LOG2E) for log in logs]
        under = 1.0 / functools.reduce(jnp.add, raised)
        weights = [jnp.concatenate([r * under, jnp.zeros((TILE - 8, TILE), jnp.float32)], 0).T for r in raised]
        for h in range(heads):
            lanes = pl.ds(h * HEAD, HEAD)
            mixed = None
            for n in range(parts):
                w = weights[n][:, h:h + 1]
                o = jnp.concatenate([tokens[n][pl.ds(r * 64 + col * 32, 32), lanes] for r in range(4)], 0)
                term = w * o.astype(jnp.float32)
                mixed = term if mixed is None else mixed + term
            mixed = mixed.astype(jnp.bfloat16)
            for r in range(4):
                out[pl.ds(r * 64 + col * 32, 32), lanes] = mixed[r * 32:(r + 1) * 32]


def call_attend(kernel, heads, place, meta, queries, keys, values, frames, longest, copies):
    width = heads * HEAD
    anywhere = pl.BlockSpec(memory_space=pl.ANY)
    smem = pl.BlockSpec(memory_space=pltpu.SMEM)
    held = pltpu.VMEM((frames, 4, 2, 32, width), jnp.bfloat16)
    square = pltpu.VMEM((heads, TILE, TILE), jnp.float32)
    return pl.pallas_call(
        functools.partial(kernel, heads),
        out_shape=[jax.ShapeDtypeStruct((ROWS + STAT, width), jnp.bfloat16)] * len(queries),
        in_specs=[smem, smem] + [anywhere] * (len(queries) + len(keys) + len(values)),
        out_specs=[pl.BlockSpec(memory_space=pltpu.VMEM)] * len(queries),
        scratch_shapes=[pltpu.VMEM((2, 4, 2, 32, width), jnp.bfloat16) for _ in queries]
        + [held, held, pltpu.SMEM((16,), jnp.int32)]
        + [pltpu.VMEM((longest, heads, TILE, TILE), jnp.float32), square, square, square]
        + [pltpu.SemaphoreType.DMA((copies,))],
        compiler_params=pltpu.CompilerParams(vmem_limit_bytes=VMEM_LIMIT),
    )(place, meta, *queries, *keys, *values)


def body(query, keys, values, selected, window_mask):
    frames, rows, cols, channels = query.shape
    heads = channels // HEAD
    shard = lax.axis_index("ta")
    height = lax.axis_index("ha")
    tx, ty = shard % SIDE, shard // SIDE
    place = jnp.stack([tx, ty, height]).astype(jnp.int32)
    q, k, v = [a.reshape(frames, rows, 2, 32, channels) for a in (query, keys, values)]
    meta = jnp.concatenate([selected.reshape(-1), window_mask.reshape(-1), jnp.zeros((META - 124,), jnp.int32)])
    meta = lax.all_gather(meta, ("ta", "ha"), tiled=True)

    right, left, up, down = along_x(1), along_x(-1), along_y(1), along_y(-1)
    kr, kl = lax.ppermute(k, "ta", right), lax.ppermute(k, "ta", left)
    vr, vl = lax.ppermute(v, "ta", right), lax.ppermute(v, "ta", left)
    ends = [(SIDE * y + 3, SIDE * y + 4) for y in range(SIDE - 1)]
    ends = ends + [(b, a) for a, b in ends]
    ke = lax.ppermute(jnp.where(tx == 0, k[0:1], k[1:2]), "ta", ends)
    ve = lax.ppermute(jnp.where(tx == 0, v[0:1], v[1:2]), "ta", ends)
    higher = [(i, i + 1) for i in range(HA - 1)]
    lower = [(b, a) for a, b in higher]
    q_low, q_high = lax.ppermute(q, "ha", higher), lax.ppermute(q, "ha", lower)
    q1, q2, q3 = lax.ppermute(q, "ta", up), lax.ppermute(q, "ta", along_y(2)), lax.ppermute(q, "ta", down)
    k2, v2 = lax.ppermute(kr, "ta", right), lax.ppermute(vl, "ta", left)

    own, for_low, for_high = call_attend(
        window_kernel, heads, place, meta, (q, q_low, q_high), (k, kr, kl, ke), (v, vr, vl, ve), 4, 6, 9
    )
    from_high = lax.ppermute(for_low, "ha", lower)
    from_low = lax.ppermute(for_high, "ha", higher)
    far_own, o1, o2, o3 = call_attend(
        far_kernel, heads, place, meta, (q, q1, q2, q3), (k, kl, k2, kr), (v, vl, v2, vr), 8, 4, 12
    )
    f1, f2, f3 = lax.ppermute(o1, "ta", down), lax.ppermute(o2, "ta", along_y(2)), lax.ppermute(o3, "ta", up)
    partial = [own, far_own, f1, f2, f3, from_low, from_high]
    out = pl.pallas_call(
        functools.partial(combine_kernel, heads, len(partial)),
        out_shape=jax.ShapeDtypeStruct((ROWS, channels), jnp.bfloat16),
        grid=(2,),
        in_specs=[pl.BlockSpec(memory_space=pltpu.SMEM)]
        + [pl.BlockSpec((256, channels), lambda f: (f, 0)) for _ in partial]
        + [pl.BlockSpec((STAT, channels), lambda f: (ROWS // STAT, 0)) for _ in partial],
        out_specs=pl.BlockSpec((256, channels), lambda f: (f, 0)),
        compiler_params=pltpu.CompilerParams(vmem_limit_bytes=VMEM_LIMIT),
    )(place, *partial, *partial)
    return out.reshape(frames, rows, cols, channels)


def solution(mesh):
    block = P("ta", "ha", None, "hd")
    table = P("ta", "ha", None, None)
    return jax.shard_map(
        body, mesh=mesh, in_specs=(block, block, block, table, table), out_specs=block, check_vma=False
    )
```

```python
import functools
import jax
import jax.numpy as jnp
import numpy as np
from jax import lax
from jax.experimental import pallas as pl
from jax.experimental.pallas import tpu as pltpu
from jax.sharding import PartitionSpec as P

HEAD = 128
TILE = 128
SEL = 4
SIDE = 4
TA = SIDE * SIDE
HA = 8
STAT = 32
TABLE = 16
CHOSEN = 32
EDGE = 8
CHUNKS = 1
NONE = -1e30
SCALE = float(HEAD ** -0.5)
LOG2E = float(np.log2(np.e))
VMEM_LIMIT = 50 * 1024 * 1024
F32 = jnp.float32
BF16 = jnp.bfloat16


def along_x(step):
    return [(SIDE * y + x, SIDE * y + (x + step) % SIDE) for y in range(SIDE) for x in range(SIDE)]


def along_y(step):
    return [(SIDE * y + x, SIDE * ((y + step) % SIDE) + x) for y in range(SIDE) for x in range(SIDE)]


def attend_tile(heads, tile, count, listed, q_ref, k_ref, v_ref, o_ref, a_ref):
    stat_rows = pl.ds(pl.multiple_of((4 * heads) * TILE + STAT * tile, STAT), STAT)

    def out_rows(h):
        return pl.ds(pl.multiple_of((tile * heads + h) * TILE, TILE), TILE)

    def score(h, keys):
        q = q_ref[tile, h]
        return lax.dot_general(keys, q, (((1,), (1,)), ((), ())), preferred_element_type=F32) * (SCALE * LOG2E)

    def pair(i, h):
        a, b = listed[2 * i], listed[2 * i + 1]
        s = score(h, jnp.concatenate([k_ref[a, h], k_ref[b, h]], 0))
        s = jnp.concatenate([s[:TILE], jnp.where(2 * i + 1 < count, s[TILE:], NONE)], 0)
        return s, jnp.concatenate([v_ref[a, h], v_ref[b, h]], 1)

    def mix(values, p):
        return jnp.dot(values, p.astype(BF16), preferred_element_type=F32)

    def write(results):
        row = lax.broadcasted_iota(jnp.int32, (8, TILE), 0)
        stats = jnp.zeros((8, TILE), F32)
        for h, (top, total, mixed) in enumerate(results):
            o_ref[out_rows(h), :] = (mixed * (1.0 / total)).astype(BF16)
            stats = jnp.where(row == h, top + jnp.log2(total), stats)
        high = stats.astype(BF16).astype(F32)
        mid = (stats - high).astype(BF16).astype(F32)
        parts = jnp.concatenate([high, mid, stats - high - mid, jnp.zeros_like(stats)], 0)
        o_ref[stat_rows, :] = parts.astype(BF16)

    def once(scores):
        results = []
        for s, v in scores:
            top = jnp.max(s, axis=0, keepdims=True)
            p = jnp.exp2(s - top)
            results.append((top, jnp.sum(p, axis=0, keepdims=True), mix(v, p)))
        write(results)

    @pl.when(count == 0)
    def _():
        for h in range(heads):
            o_ref[out_rows(h), :] = jnp.zeros((TILE, TILE), BF16)
        row = lax.broadcasted_iota(jnp.int32, (STAT, TILE), 0)
        o_ref[stat_rows, :] = jnp.where(row < 8, NONE, 0.0).astype(BF16)

    @pl.when(count == 1)
    def _():
        once([(score(h, k_ref[listed[0], h]), v_ref[listed[0], h]) for h in range(heads)])

    @pl.when(count == 2)
    def _():
        once([pair(0, h) for h in range(heads)])

    @pl.when(count > 2)
    def _():
        for h in range(heads):
            a_ref[h] = jnp.zeros((TILE, TILE), F32)

        def step(i, carry):
            after = []
            for h in range(heads):
                top, total = carry[h]
                s, v = pair(i, h)
                higher = jnp.maximum(top, jnp.max(s, axis=0, keepdims=True))
                fade = jnp.exp2(top - higher)
                p = jnp.exp2(s - higher)
                a_ref[h] = a_ref[h] * fade + mix(v, p)
                after.append((higher, total * fade + jnp.sum(p, axis=0, keepdims=True)))
            return tuple(after)

        start = ((jnp.full((1, TILE), NONE, F32), jnp.zeros((1, TILE), F32)),) * heads
        ends = lax.fori_loop(0, (count + 1) // 2, step, start)
        write([(top, total, a_ref[h]) for h, (top, total) in enumerate(ends)])


def attend_kernel(heads, chunk, sets, pieces, edged, earlier, place, *refs):
    refs = list(refs)
    queries = [refs.pop(0) for _ in sets]
    held = [[refs.pop(0), refs.pop(0)] if piece else None for piece in pieces]
    edge = refs.pop(0) if edged else None
    del refs[:earlier]
    outs = [refs.pop(0) for _ in sets]
    q_bufs = [refs.pop(0) for _ in sets]
    kb, vb, marks, ints, table, listed, a_ref, sems, table_sem = refs
    tx, ty, height = place[0], place[1], place[2]
    shard = ty * SIDE + tx
    copies = []

    def copy(src, dst):
        c = pltpu.make_async_copy(src, dst, sems.at[len(copies)])
        c.start()
        copies.append(c)

    for n, (src, dst) in enumerate(zip(queries, q_bufs)):
        copy(src.at[4, 0, pl.ds(0, TABLE)], marks.at[n])
    for src, dst in zip(queries, q_bufs):
        copy(src.at[pl.ds(0, 4), pl.ds(chunk * heads, heads)], dst)
    for n, piece in enumerate(pieces):
        if piece:
            first, many = piece
            for m, dst in enumerate((kb, vb)):
                src = held[n][m]
                src = src.at[m] if len(src.shape) == 5 else src
                copy(src.at[pl.ds(2 * first, 2 * many)], dst.at[pl.ds(2 * (2 * n + first), 2 * many)])
    if edged:
        for m, dst in enumerate((kb, vb)):
            copy(edge.at[m, :, pl.ds(chunk * heads, heads)], dst.at[pl.ds(2 * EDGE, 2)])
    for c in copies[:len(sets)]:
        c.wait()
    for n in range(len(sets)):
        ints[pl.ds(8 * n, 8), :] = marks[n].astype(F32)[0:8].astype(jnp.int32)
    tables = pltpu.make_async_copy(ints, table, table_sem)
    tables.start()
    tables.wait()
    for c in copies[len(sets):]:
        c.wait()

    for n, (dh, window, far) in enumerate(sets):
        asker = height - dh
        there = (asker >= 0) & (asker < HA)

        def one_tile(tile, carry):
            frame, col = tile // 2, tile % 2
            count = jnp.int32(0)
            if window:
                for df in range(3):
                    near = 2 * shard + frame + df - 1
                    inside = there & (near >= 0) & (near < 2 * TA)
                    at = 2 * tx + frame + df - 1
                    piece = (at + 2 * SIDE) // 2 - tx
                    slot = 2 * (piece & (SIDE - 1)) + (at & 1)
                    slot = jnp.where((at < 0) | (at >= 2 * SIDE), EDGE, slot)
                    for kw in range(2):
                        number = df * 9 + (dh + 1) * 3 + (kw - col + 1)
                        used = (table[8 * n + tile, number] == 1) | ((dh == 0) & (number == 13))
                        listed[count] = slot * 2 + kw
                        count = count + (used & inside).astype(jnp.int32)
            if far:
                for j in range(SEL):
                    owner = table[8 * n + tile, CHOSEN + j]
                    piece = (owner + SIDE - tx) & (SIDE - 1)
                    listed[count] = (piece * 2 + frame) * 2 + col
                    count = count + (owner // SIDE == ty).astype(jnp.int32)
            listed[count] = listed[0]
            attend_tile(heads, tile, count, listed, q_bufs[n], kb, vb, outs[n], a_ref)
            return carry

        lax.fori_loop(0, 4, one_tile, 0)


def call_attend(heads, chunk, place, sets, queries, pieces, held, edge, earlier=()):
    anywhere = pl.BlockSpec(memory_space=pl.ANY)
    smem = pl.BlockSpec(memory_space=pltpu.SMEM)
    keys = pltpu.VMEM((18, heads, TILE, TILE), BF16)
    operands = list(queries)
    for piece, pair in zip(pieces, held):
        operands += list(pair) if piece else []
    operands += [] if edge is None else [edge]
    operands += list(earlier)
    count = 2 * len(sets) + 2 * sum(piece is not None for piece in pieces) + 2 * (edge is not None)
    rows = 4 * (heads * TILE + STAT)
    return pl.pallas_call(
        functools.partial(attend_kernel, heads, chunk, sets, pieces, edge is not None, len(earlier)),
        out_shape=[jax.ShapeDtypeStruct((rows, TILE), BF16)] * len(sets),
        in_specs=[smem] + [anywhere] * len(operands),
        out_specs=[pl.BlockSpec(memory_space=pltpu.VMEM)] * len(sets),
        scratch_shapes=[pltpu.VMEM((4, heads, TILE, TILE), BF16) for _ in sets]
        + [keys, keys, pltpu.VMEM((len(sets), TABLE, TILE), BF16)]
        + [pltpu.VMEM((8 * len(sets), TILE), jnp.int32), pltpu.SMEM((8 * len(sets), TILE), jnp.int32)]
        + [pltpu.SMEM((16,), jnp.int32), pltpu.VMEM((heads, TILE, TILE), F32)]
        + [pltpu.SemaphoreType.DMA((count,)), pltpu.SemaphoreType.DMA],
        compiler_params=pltpu.CompilerParams(vmem_limit_bytes=VMEM_LIMIT),
    )(place, *operands)


def arrange_kernel(heads, place, chosen, window, q_in, k_in, v_in, *refs):
    outs, (q, k, v, marks, sems) = refs[:-5], refs[-5:]
    q_out, edge, both = outs[0], outs[1], outs[2:]
    copies = [pltpu.make_async_copy(src, dst, sems.at[n]) for n, (src, dst) in enumerate(((k_in, k), (v_in, v), (q_in, q)))]
    for c in copies:
        c.start()
    marks[...] = jnp.zeros_like(marks)
    marks[pl.ds(0, 4), pl.ds(0, 27)] = window[...].astype(F32)
    marks[pl.ds(0, 4), pl.ds(CHOSEN, SEL)] = chosen[...].astype(F32)
    q_out[4, 0, pl.ds(0, TABLE)] = marks[...].astype(BF16)
    per = heads // CHUNKS
    tiles = [(tile, h, h // per, h % per, pl.ds(h * HEAD, HEAD)) for tile in range(4) for h in range(heads)]
    copies[0].wait()
    for tile, h, chunk, at, lanes in tiles:
        both[chunk][0, tile, at] = k[tile // 2, :, tile % 2, :, lanes].reshape(TILE, HEAD)
    copies[1].wait()
    for tile, h, chunk, at, lanes in tiles:
        both[chunk][1, tile, at] = v[tile // 2, :, tile % 2, :, lanes].reshape(TILE, HEAD).T
    copies[2].wait()
    for tile, h, chunk, at, lanes in tiles:
        q_out[tile, h] = q[tile // 2, :, tile % 2, :, lanes].reshape(TILE, HEAD)
    first = jnp.where(place[0] == 0, 0, 2)
    for chunk in range(CHUNKS):
        for n in range(2):
            for col in range(2):
                edge[n, col, pl.ds(chunk * per, per)] = both[chunk][n, first + col]


def tie_kernel(*refs):
    del refs


def tie(arrays, earlier):
    anywhere = pl.BlockSpec(memory_space=pl.ANY)
    return pl.pallas_call(
        tie_kernel,
        out_shape=[jax.ShapeDtypeStruct(a.shape, a.dtype) for a in arrays],
        in_specs=[anywhere] * (len(arrays) + len(earlier)),
        out_specs=[anywhere] * len(arrays),
        input_output_aliases={n: n for n in range(len(arrays))},
    )(*arrays, *earlier)


def combine_kernel(heads, parts, place, *refs):
    sources, out = refs[:-1], refs[-1]
    height = place[2]
    there = {parts - 2: height > 0, parts - 1: height < HA - 1}
    for chunk in range(CHUNKS):
        mine = sources[chunk * 2 * parts:(chunk + 1) * 2 * parts]
        tokens, stats = mine[:parts], mine[parts:]
        logs = []
        for n in range(parts):
            s = stats[n][...].astype(F32)
            log = s[0:8] + s[8:16] + s[16:24]
            logs.append(jnp.where(there[n], log, NONE) if n in there else log)
        top = functools.reduce(jnp.maximum, logs)
        raised = [jnp.exp2(log - top) for log in logs]
        under = 1.0 / functools.reduce(jnp.add, raised)
        weights = [r * under for r in raised]
        for h in range(heads):
            terms = [weights[n][h:h + 1] * tokens[n][pl.ds(h * TILE, TILE), :].astype(F32) for n in range(parts)]
            mixed = functools.reduce(jnp.add, terms).T.astype(BF16)
            lanes = pl.ds((chunk * heads + h) * HEAD, HEAD)
            out[0, :, 0, :, lanes] = mixed.reshape(4, 32, HEAD)


def body(query, keys, values, selected, window_mask):
    frames, rows, cols, channels = query.shape
    heads = channels // HEAD // CHUNKS
    shard = lax.axis_index("ta")
    height = lax.axis_index("ha")
    tx, ty = shard % SIDE, shard // SIDE
    place = jnp.stack([tx, ty, height]).astype(jnp.int32)
    right, left, up, down = along_x(1), along_x(-1), along_y(1), along_y(-1)
    opposite = along_y(2)
    ends = [(SIDE * y + 3, SIDE * y + 4) for y in range(SIDE - 1)]
    ends = ends + [(b, a) for a, b in ends]
    higher = [(i, i + 1) for i in range(HA - 1)]
    lower = [(b, a) for a, b in higher]

    def permute(array, pairs, axis="ta"):
        return lax.ppermute(array, axis, pairs)

    smem, vmem, anywhere = [pl.BlockSpec(memory_space=m) for m in (pltpu.SMEM, pltpu.VMEM, pl.ANY)]
    blocks = [a.reshape(frames, rows, 2, 32, channels) for a in (query, keys, values)]
    q, edge, *both = pl.pallas_call(
        functools.partial(arrange_kernel, heads * CHUNKS),
        out_shape=[jax.ShapeDtypeStruct((5, heads * CHUNKS, TILE, TILE), BF16)]
        + [jax.ShapeDtypeStruct((2, 2, heads * CHUNKS, TILE, TILE), BF16)]
        + [jax.ShapeDtypeStruct((2, 4, heads, TILE, TILE), BF16)] * CHUNKS,
        in_specs=[smem, vmem, vmem] + [anywhere] * 3,
        out_specs=[vmem] * (2 + CHUNKS),
        scratch_shapes=[pltpu.VMEM(blocks[0].shape, BF16) for _ in range(3)]
        + [pltpu.VMEM((TABLE, TILE), F32), pltpu.SemaphoreType.DMA((3,))],
        compiler_params=pltpu.CompilerParams(vmem_limit_bytes=60 * 1024 * 1024),
    )(place, selected.reshape(4, SEL), window_mask.reshape(4, 27), *blocks)

    from_left = [permute(b, right) for b in both]
    from_right = [permute(b, left) for b in both]
    far_k = [permute(b[0], right) for b in from_left]
    far_v = [permute(b[1], left) for b in from_right]
    q1, q3 = permute(q, up), permute(q, down)
    q_low = permute(q, higher, "ha")
    again, edge = tie((q, edge), (q1, q3, q_low))
    q_high = permute(again, lower, "ha")
    q2 = permute(again, opposite)
    edge = permute(edge, ends)

    partial = []
    whole = ((0, 2),) * SIDE
    for c in range(CHUNKS):
        held = ((both[c],) * 2, (from_right[c],) * 2, (far_k[c], far_v[c]), (from_left[c],) * 2)
        for_low, for_high = call_attend(
            heads, c, place, ((1, True, False), (-1, True, False)), (q_low, q_high),
            ((0, 2), (0, 1), None, (1, 1)), held, edge,
        )
        o1, o2, o3 = call_attend(heads, c, place, ((0, False, True),) * 3, (q1, q2, q3), whole, held, None)
        f2, f1, f3 = permute(o2, opposite), permute(o1, down), permute(o3, up)
        for_low, for_high = tie((for_low, for_high), (o1,))
        from_high, from_low = permute(for_low, lower, "ha"), permute(for_high, higher, "ha")
        (mine,) = call_attend(heads, c, place, ((0, True, True),), (q,), whole, held, edge, (o1,))
        partial.append([mine, f1, f2, f3, from_low, from_high])

    count = len(partial[0])
    token_spec = pl.BlockSpec((heads * TILE, TILE), lambda t: (t, 0))
    stat_spec = pl.BlockSpec((STAT, TILE), lambda t: (4 * heads * TILE // STAT + t, 0))
    out = pl.pallas_call(
        functools.partial(combine_kernel, heads, count),
        out_shape=jax.ShapeDtypeStruct((frames, rows, 2, 32, channels), BF16),
        grid=(4,),
        in_specs=[pl.BlockSpec(memory_space=pltpu.SMEM)] + ([token_spec] * count + [stat_spec] * count) * CHUNKS,
        out_specs=pl.BlockSpec((1, rows, 1, 32, channels), lambda t: (t // 2, 0, t % 2, 0, 0)),
        compiler_params=pltpu.CompilerParams(vmem_limit_bytes=VMEM_LIMIT),
    )(place, *[a for some in partial for a in some + some])
    return out.reshape(frames, rows, cols, channels)


def solution(mesh):
    block = P("ta", "ha", None, "hd")
    table = P("ta", "ha", None, None)
    return jax.shard_map(
        body, mesh=mesh, in_specs=(block, block, block, table, table), out_specs=block, check_vma=False
    )
```

```python
import functools
import jax
import jax.numpy as jnp
import numpy as np
from jax import lax
from jax.experimental import pallas as pl
from jax.experimental.pallas import tpu as pltpu
from jax.sharding import PartitionSpec as P

HEAD = 128
TILE = 128
SEL = 4
SIDE = 4
TA = SIDE * SIDE
HA = 8
STAT = 32
TABLE = 16
CHOSEN = 32
EDGE = 8
CHUNKS = 1
NONE = -1e30
SCALE = float(HEAD ** -0.5)
LOG2E = float(np.log2(np.e))
VMEM_LIMIT = 60 * 1024 * 1024
F32 = jnp.float32
BF16 = jnp.bfloat16


def along_x(step):
    return [(SIDE * y + x, SIDE * y + (x + step) % SIDE) for y in range(SIDE) for x in range(SIDE)]


def along_y(step):
    return [(SIDE * y + x, SIDE * ((y + step) % SIDE) + x) for y in range(SIDE) for x in range(SIDE)]


def attend_tile(heads, tile, count, listed, q_ref, k_ref, v_ref, o_ref, a_ref):
    stat_rows = pl.ds(pl.multiple_of((4 * heads) * TILE + STAT * tile, STAT), STAT)

    def out_rows(h):
        return pl.ds(pl.multiple_of((tile * heads + h) * TILE, TILE), TILE)

    def score(h, keys):
        q = q_ref[tile, h]
        return lax.dot_general(keys, q, (((1,), (1,)), ((), ())), preferred_element_type=F32) * (SCALE * LOG2E)

    def pair(i, h):
        a, b = listed[2 * i], listed[2 * i + 1]
        s = score(h, jnp.concatenate([k_ref[a, h], k_ref[b, h]], 0))
        s = jnp.concatenate([s[:TILE], jnp.where(2 * i + 1 < count, s[TILE:], NONE)], 0)
        return s, jnp.concatenate([v_ref[a, h], v_ref[b, h]], 1)

    def mix(values, p):
        return jnp.dot(values, p.astype(BF16), preferred_element_type=F32)

    def write(results):
        row = lax.broadcasted_iota(jnp.int32, (8, TILE), 0)
        stats = jnp.zeros((8, TILE), F32)
        for h, (top, total, mixed) in enumerate(results):
            o_ref[out_rows(h), :] = (mixed * (1.0 / total)).astype(BF16)
            stats = jnp.where(row == h, top + jnp.log2(total), stats)
        high = stats.astype(BF16).astype(F32)
        mid = (stats - high).astype(BF16).astype(F32)
        parts = jnp.concatenate([high, mid, stats - high - mid, jnp.zeros_like(stats)], 0)
        o_ref[stat_rows, :] = parts.astype(BF16)

    def once(scores):
        results = []
        for s, v in scores:
            top = jnp.max(s, axis=0, keepdims=True)
            p = jnp.exp2(s - top)
            results.append((top, jnp.sum(p, axis=0, keepdims=True), mix(v, p)))
        write(results)

    @pl.when(count == 0)
    def _():
        for h in range(heads):
            o_ref[out_rows(h), :] = jnp.zeros((TILE, TILE), BF16)
        row = lax.broadcasted_iota(jnp.int32, (STAT, TILE), 0)
        o_ref[stat_rows, :] = jnp.where(row < 8, NONE, 0.0).astype(BF16)

    @pl.when(count == 1)
    def _():
        once([(score(h, k_ref[listed[0], h]), v_ref[listed[0], h]) for h in range(heads)])

    @pl.when(count == 2)
    def _():
        once([pair(0, h) for h in range(heads)])

    @pl.when(count > 2)
    def _():
        for h in range(heads):
            a_ref[h] = jnp.zeros((TILE, TILE), F32)

        def step(i, carry):
            after = []
            for h in range(heads):
                top, total = carry[h]
                s, v = pair(i, h)
                higher = jnp.maximum(top, jnp.max(s, axis=0, keepdims=True))
                fade = jnp.exp2(top - higher)
                p = jnp.exp2(s - higher)
                a_ref[h] = a_ref[h] * fade + mix(v, p)
                after.append((higher, total * fade + jnp.sum(p, axis=0, keepdims=True)))
            return tuple(after)

        start = ((jnp.full((1, TILE), NONE, F32), jnp.zeros((1, TILE), F32)),) * heads
        ends = lax.fori_loop(0, (count + 1) // 2, step, start)
        write([(top, total, a_ref[h]) for h, (top, total) in enumerate(ends)])


def attend_kernel(heads, chunk, sets, pieces, edged, earlier, together, place, *refs):
    refs = list(refs)
    queries = [refs.pop(0) for _ in sets]
    held = [[refs.pop(0), refs.pop(0)] if piece else None for piece in pieces]
    edge = refs.pop(0) if edged else None
    del refs[:earlier]
    outs = [refs.pop(0) for _ in range(1 if together else len(sets))]
    q_bufs = [refs.pop(0) for _ in sets]
    kb, vb, marks, ints, table, listed, a_ref, sems, table_sem = refs
    tx, ty, height = place[0], place[1], place[2]
    shard = ty * SIDE + tx
    if together:
        outs = [outs[0].at[(ty + SIDE - n) & (SIDE - 1)] for n in range(SIDE)]
    copies = []

    def copy(src, dst):
        c = pltpu.make_async_copy(src, dst, sems.at[len(copies)])
        c.start()
        copies.append(c)

    for n, (src, dst) in enumerate(zip(queries, q_bufs)):
        copy(src.at[4, 0, pl.ds(0, TABLE)], marks.at[n])
    for src, dst in zip(queries, q_bufs):
        copy(src.at[pl.ds(0, 4), pl.ds(chunk * heads, heads)], dst)
    for n, piece in enumerate(pieces):
        if piece:
            first, many = piece
            for m, dst in enumerate((kb, vb)):
                src = held[n][m]
                src = src.at[m] if len(src.shape) == 5 else src
                copy(src.at[pl.ds(2 * first, 2 * many)], dst.at[pl.ds(2 * (2 * n + first), 2 * many)])
    if edged:
        for m, dst in enumerate((kb, vb)):
            copy(edge.at[m, :, pl.ds(chunk * heads, heads)], dst.at[pl.ds(2 * EDGE, 2)])
    for c in copies[:len(sets)]:
        c.wait()
    for n in range(len(sets)):
        ints[pl.ds(8 * n, 8), :] = marks[n].astype(F32)[0:8].astype(jnp.int32)
    tables = pltpu.make_async_copy(ints, table, table_sem)
    tables.start()
    tables.wait()
    for c in copies[len(sets):]:
        c.wait()

    for n, (dh, window, far) in enumerate(sets):
        asker = height - dh
        there = (asker >= 0) & (asker < HA)

        def one_tile(tile, carry):
            frame, col = tile // 2, tile % 2
            count = jnp.int32(0)
            if window:
                for df in range(3):
                    near = 2 * shard + frame + df - 1
                    inside = there & (near >= 0) & (near < 2 * TA)
                    at = 2 * tx + frame + df - 1
                    piece = (at + 2 * SIDE) // 2 - tx
                    slot = 2 * (piece & (SIDE - 1)) + (at & 1)
                    slot = jnp.where((at < 0) | (at >= 2 * SIDE), EDGE, slot)
                    for kw in range(2):
                        number = df * 9 + (dh + 1) * 3 + (kw - col + 1)
                        used = (table[8 * n + tile, number] == 1) | ((dh == 0) & (number == 13))
                        listed[count] = slot * 2 + kw
                        count = count + (used & inside).astype(jnp.int32)
            if far:
                for j in range(SEL):
                    owner = table[8 * n + tile, CHOSEN + j]
                    piece = (owner + SIDE - tx) & (SIDE - 1)
                    listed[count] = (piece * 2 + frame) * 2 + col
                    count = count + (owner // SIDE == ty).astype(jnp.int32)
            listed[count] = listed[0]
            attend_tile(heads, tile, count, listed, q_bufs[n], kb, vb, outs[n], a_ref)
            return carry

        lax.fori_loop(0, 4, one_tile, 0)


def call_attend(heads, chunk, place, sets, queries, pieces, held, edge, earlier=(), together=False):
    anywhere = pl.BlockSpec(memory_space=pl.ANY)
    smem = pl.BlockSpec(memory_space=pltpu.SMEM)
    keys = pltpu.VMEM((18, heads, TILE, TILE), BF16)
    operands = list(queries)
    for piece, pair in zip(pieces, held):
        operands += list(pair) if piece else []
    operands += [] if edge is None else [edge]
    operands += list(earlier)
    count = 2 * len(sets) + 2 * sum(piece is not None for piece in pieces) + 2 * (edge is not None)
    rows = 4 * (heads * TILE + STAT)
    return pl.pallas_call(
        functools.partial(attend_kernel, heads, chunk, sets, pieces, edge is not None, len(earlier), together),
        out_shape=[jax.ShapeDtypeStruct((SIDE, rows, TILE), BF16)]
        if together
        else [jax.ShapeDtypeStruct((rows, TILE), BF16)] * len(sets),
        in_specs=[smem] + [anywhere] * len(operands),
        out_specs=[pl.BlockSpec(memory_space=pltpu.VMEM)] * (1 if together else len(sets)),
        scratch_shapes=[pltpu.VMEM((4, heads, TILE, TILE), BF16) for _ in sets]
        + [keys, keys, pltpu.VMEM((len(sets), TABLE, TILE), BF16)]
        + [pltpu.VMEM((8 * len(sets), TILE), jnp.int32), pltpu.SMEM((8 * len(sets), TILE), jnp.int32)]
        + [pltpu.SMEM((16,), jnp.int32), pltpu.VMEM((heads, TILE, TILE), F32)]
        + [pltpu.SemaphoreType.DMA((count,)), pltpu.SemaphoreType.DMA],
        compiler_params=pltpu.CompilerParams(vmem_limit_bytes=VMEM_LIMIT),
    )(place, *operands)


def arrange_kernel(heads, chosen, window, q_in, k_in, v_in, *refs):
    outs, (q, k, v, marks, sems) = refs[:-5], refs[-5:]
    q_out, both = outs[0], outs[1:]
    copies = [pltpu.make_async_copy(src, dst, sems.at[n]) for n, (src, dst) in enumerate(((k_in, k), (v_in, v), (q_in, q)))]
    for c in copies:
        c.start()
    marks[...] = jnp.zeros_like(marks)
    marks[pl.ds(0, 4), pl.ds(0, 27)] = window[...].astype(F32)
    marks[pl.ds(0, 4), pl.ds(CHOSEN, SEL)] = chosen[...].astype(F32)
    q_out[4, 0, pl.ds(0, TABLE)] = marks[...].astype(BF16)
    per = heads // CHUNKS
    tiles = [(tile, h, h // per, h % per, pl.ds(h * HEAD, HEAD)) for tile in range(4) for h in range(heads)]
    copies[0].wait()
    for tile, h, chunk, at, lanes in tiles:
        both[chunk][0, tile, at] = k[tile // 2, :, tile % 2, :, lanes].reshape(TILE, HEAD)
    copies[1].wait()
    for tile, h, chunk, at, lanes in tiles:
        both[chunk][1, tile, at] = v[tile // 2, :, tile % 2, :, lanes].reshape(TILE, HEAD).T
    copies[2].wait()
    for tile, h, chunk, at, lanes in tiles:
        q_out[tile, h] = q[tile // 2, :, tile % 2, :, lanes].reshape(TILE, HEAD)


def tie_kernel(*refs):
    del refs


def tie(arrays, earlier):
    anywhere = pl.BlockSpec(memory_space=pl.ANY)
    return pl.pallas_call(
        tie_kernel,
        out_shape=[jax.ShapeDtypeStruct(a.shape, a.dtype) for a in arrays],
        in_specs=[anywhere] * (len(arrays) + len(earlier)),
        out_specs=[anywhere] * len(arrays),
        input_output_aliases={n: n for n in range(len(arrays))},
    )(*arrays, *earlier)


def combine_kernel(heads, parts, place, *refs):
    sources, out = refs[:-1], refs[-1]
    height = place[2]
    there = {parts - 2: height > 0, parts - 1: height < HA - 1}
    for chunk in range(CHUNKS):
        mine = sources[chunk * 2 * parts:(chunk + 1) * 2 * parts]
        tokens, stats = mine[:parts], mine[parts:]
        logs = []
        for n in range(parts):
            s = stats[n][...].astype(F32)
            log = s[0:8] + s[8:16] + s[16:24]
            logs.append(jnp.where(there[n], log, NONE) if n in there else log)
        top = functools.reduce(jnp.maximum, logs)
        raised = [jnp.exp2(log - top) for log in logs]
        under = 1.0 / functools.reduce(jnp.add, raised)
        weights = [r * under for r in raised]
        for h in range(heads):
            terms = [weights[n][h:h + 1] * tokens[n][pl.ds(h * TILE, TILE), :].astype(F32) for n in range(parts)]
            mixed = functools.reduce(jnp.add, terms).T.astype(BF16)
            lanes = pl.ds((chunk * heads + h) * HEAD, HEAD)
            out[0, :, 0, :, lanes] = mixed.reshape(4, 32, HEAD)


def body(query, keys, values, selected, window_mask):
    frames, rows, cols, channels = query.shape
    heads = channels // HEAD // CHUNKS
    shard = lax.axis_index("ta")
    height = lax.axis_index("ha")
    tx, ty = shard % SIDE, shard // SIDE
    place = jnp.stack([tx, ty, height]).astype(jnp.int32)
    right, left, up, down = along_x(1), along_x(-1), along_y(1), along_y(-1)
    opposite = along_y(2)
    columns = [[SIDE * y + x for y in range(SIDE)] for x in range(SIDE)]
    ends = [(SIDE * y, SIDE * y + SIDE) for y in range(SIDE - 1)]
    ends = ends + [(SIDE * y + SIDE + 3, SIDE * y + 3) for y in range(SIDE - 1)]
    higher = [(i, i + 1) for i in range(HA - 1)]
    lower = [(b, a) for a, b in higher]

    def permute(array, pairs, axis="ta"):
        return lax.ppermute(array, axis, pairs)

    vmem, anywhere = [pl.BlockSpec(memory_space=m) for m in (pltpu.VMEM, pl.ANY)]
    blocks = [a.reshape(frames, rows, 2, 32, channels) for a in (query, keys, values)]
    q, *both = pl.pallas_call(
        functools.partial(arrange_kernel, heads * CHUNKS),
        out_shape=[jax.ShapeDtypeStruct((5, heads * CHUNKS, TILE, TILE), BF16)]
        + [jax.ShapeDtypeStruct((2, 4, heads, TILE, TILE), BF16)] * CHUNKS,
        in_specs=[vmem, vmem] + [anywhere] * 3,
        out_specs=[vmem] * (1 + CHUNKS),
        scratch_shapes=[pltpu.VMEM(blocks[0].shape, BF16) for _ in range(3)]
        + [pltpu.VMEM((TABLE, TILE), F32), pltpu.SemaphoreType.DMA((3,))],
        compiler_params=pltpu.CompilerParams(vmem_limit_bytes=VMEM_LIMIT),
    )(selected.reshape(4, SEL), window_mask.reshape(4, 27), *blocks)

    q1, q2, q3 = permute(q, up), permute(q, opposite), permute(q, down)
    (q,) = tie((q,), (q1, q3))
    q_low, q_high = permute(q, higher, "ha"), permute(q, lower, "ha")
    from_left, from_right = [], []
    for c in range(CHUNKS):
        if c:
            (both[c],) = tie((both[c],), (from_left[-1], from_right[-1]))
        from_left.append(permute(both[c], right))
        from_right.append(permute(both[c], left))
    far_k = [permute(b[0], right) for b in from_left]
    far_v = [permute(b[1], left) for b in from_right]
    edge = [jnp.where(tx == 0, a[:, 2:], b[:, :2]) for a, b in zip(from_left, from_right)]
    edge = permute(jnp.concatenate(edge, 2), ends)

    partial = []
    whole = ((0, 2),) * SIDE
    for c in range(CHUNKS):
        held = ((both[c],) * 2, (from_right[c],) * 2, (far_k[c], far_v[c]), (from_left[c],) * 2)
        far_sets = ((0, False, True),) * SIDE
        (parts,) = call_attend(heads, c, place, far_sets, (q, q1, q2, q3), whole, held, None, (edge,), True)
        arrived = lax.all_to_all(parts, "ta", 0, 0, axis_index_groups=columns, tiled=True)
        near = ((0, 2), (0, 1), None, (1, 1))
        for_low, for_high = call_attend(
            heads, c, place, ((1, True, False), (-1, True, False)), (q_low, q_high), near, held, edge, (parts,)
        )
        from_high, from_low = permute(for_low, lower, "ha"), permute(for_high, higher, "ha")
        (mine,) = call_attend(heads, c, place, ((0, True, False),), (q,), near, held, edge, (for_low,))
        partial.append([arrived] * SIDE + [mine, from_low, from_high])

    count = len(partial[0])
    tokens, stats = [], []
    for n in range(count):
        lead, at = ((None,), (n,)) if n < SIDE else ((), ())
        tokens.append(pl.BlockSpec(lead + (heads * TILE, TILE), lambda t, at=at: at + (t, 0)))
        stats.append(pl.BlockSpec(lead + (STAT, TILE), lambda t, at=at: at + (4 * heads * TILE // STAT + t, 0)))
    out = pl.pallas_call(
        functools.partial(combine_kernel, heads, count),
        out_shape=jax.ShapeDtypeStruct((frames, rows, 2, 32, channels), BF16),
        grid=(4,),
        in_specs=[pl.BlockSpec(memory_space=pltpu.SMEM)] + (tokens + stats) * CHUNKS,
        out_specs=pl.BlockSpec((1, rows, 1, 32, channels), lambda t: (t // 2, 0, t % 2, 0, 0)),
        compiler_params=pltpu.CompilerParams(vmem_limit_bytes=VMEM_LIMIT),
    )(place, *[a for some in partial for a in some + some])
    return out.reshape(frames, rows, cols, channels)


def solution(mesh):
    block = P("ta", "ha", None, "hd")
    table = P("ta", "ha", None, None)
    return jax.shard_map(
        body, mesh=mesh, in_specs=(block, block, block, table, table), out_specs=block, check_vma=False
    )
```

```python
import functools
import jax
import jax.numpy as jnp
import numpy as np
from jax import lax
from jax.experimental import pallas as pl
from jax.experimental.pallas import tpu as pltpu
from jax.sharding import PartitionSpec as P

HEAD = 128
TILE = 128
SEL = 4
SIDE = 4
TA = SIDE * SIDE
HA = 8
STAT = 32
TABLE = 16
CHOSEN = 32
EDGE = 8
CHUNKS = 1
NONE = -1e30
SCALE = float(HEAD ** -0.5)
LOG2E = float(np.log2(np.e))
VMEM_LIMIT = 60 * 1024 * 1024
F32 = jnp.float32
BF16 = jnp.bfloat16


def along_x(step):
    return [(SIDE * y + x, SIDE * y + (x + step) % SIDE) for y in range(SIDE) for x in range(SIDE)]


def along_y(step):
    return [(SIDE * y + x, SIDE * ((y + step) % SIDE) + x) for y in range(SIDE) for x in range(SIDE)]


def attend_tile(heads, tile, count, listed, q_ref, k_ref, v_ref, o_ref, a_ref):
    stat_rows = pl.ds(pl.multiple_of((4 * heads) * TILE + STAT * tile, STAT), STAT)

    def out_rows(h):
        return pl.ds(pl.multiple_of((tile * heads + h) * TILE, TILE), TILE)

    def score(h, keys):
        q = q_ref[tile, h]
        return lax.dot_general(keys, q, (((1,), (1,)), ((), ())), preferred_element_type=F32) * (SCALE * LOG2E)

    def pair(i, h):
        a, b = listed[2 * i], listed[2 * i + 1]
        s = score(h, jnp.concatenate([k_ref[a, h], k_ref[b, h]], 0))
        s = jnp.concatenate([s[:TILE], jnp.where(2 * i + 1 < count, s[TILE:], NONE)], 0)
        return s, jnp.concatenate([v_ref[a, h], v_ref[b, h]], 1)

    def mix(values, p):
        return jnp.dot(values, p.astype(BF16), preferred_element_type=F32)

    def write(results):
        row = lax.broadcasted_iota(jnp.int32, (8, TILE), 0)
        stats = jnp.zeros((8, TILE), F32)
        for h, (top, total, mixed) in enumerate(results):
            o_ref[out_rows(h), :] = (mixed * (1.0 / total)).astype(BF16)
            stats = jnp.where(row == h, top + jnp.log2(total), stats)
        high = stats.astype(BF16).astype(F32)
        mid = (stats - high).astype(BF16).astype(F32)
        parts = jnp.concatenate([high, mid, stats - high - mid, jnp.zeros_like(stats)], 0)
        o_ref[stat_rows, :] = parts.astype(BF16)

    def once(scores):
        results = []
        for s, v in scores:
            top = jnp.max(s, axis=0, keepdims=True)
            p = jnp.exp2(s - top)
            results.append((top, jnp.sum(p, axis=0, keepdims=True), mix(v, p)))
        write(results)

    @pl.when(count == 0)
    def _():
        for h in range(heads):
            o_ref[out_rows(h), :] = jnp.zeros((TILE, TILE), BF16)
        row = lax.broadcasted_iota(jnp.int32, (STAT, TILE), 0)
        o_ref[stat_rows, :] = jnp.where(row < 8, NONE, 0.0).astype(BF16)

    @pl.when(count == 1)
    def _():
        once([(score(h, k_ref[listed[0], h]), v_ref[listed[0], h]) for h in range(heads)])

    @pl.when(count == 2)
    def _():
        once([pair(0, h) for h in range(heads)])

    @pl.when(count > 2)
    def _():
        for h in range(heads):
            a_ref[h] = jnp.zeros((TILE, TILE), F32)

        def step(i, carry):
            after = []
            for h in range(heads):
                top, total = carry[h]
                s, v = pair(i, h)
                higher = jnp.maximum(top, jnp.max(s, axis=0, keepdims=True))
                fade = jnp.exp2(top - higher)
                p = jnp.exp2(s - higher)
                a_ref[h] = a_ref[h] * fade + mix(v, p)
                after.append((higher, total * fade + jnp.sum(p, axis=0, keepdims=True)))
            return tuple(after)

        start = ((jnp.full((1, TILE), NONE, F32), jnp.zeros((1, TILE), F32)),) * heads
        ends = lax.fori_loop(0, (count + 1) // 2, step, start)
        write([(top, total, a_ref[h]) for h, (top, total) in enumerate(ends)])


def attend_kernel(heads, chunk, sets, pieces, edged, earlier, together, place, *refs):
    refs = list(refs)
    queries = [refs.pop(0) for _ in sets]
    held = [[refs.pop(0), refs.pop(0)] if piece else None for piece in pieces]
    edge = refs.pop(0) if edged else None
    del refs[:earlier]
    outs = [refs.pop(0) for _ in range(1 if together else len(sets))]
    q_bufs = [refs.pop(0) for _ in sets]
    kb, vb, marks, ints, table, listed, a_ref, sems, table_sem = refs
    tx, ty, height = place[0], place[1], place[2]
    shard = ty * SIDE + tx
    if together:
        outs = [outs[0].at[(ty + SIDE - n) & (SIDE - 1)] for n in range(SIDE)]
    copies = []

    def copy(src, dst):
        c = pltpu.make_async_copy(src, dst, sems.at[len(copies)])
        c.start()
        copies.append(c)

    for n, (src, dst) in enumerate(zip(queries, q_bufs)):
        copy(src.at[4, 0, pl.ds(0, TABLE)], marks.at[n])
    for src, dst in zip(queries, q_bufs):
        copy(src.at[pl.ds(0, 4), pl.ds(chunk * heads, heads)], dst)
    for n, piece in enumerate(pieces):
        if piece:
            first, many = piece
            for m, dst in enumerate((kb, vb)):
                src = held[n][m]
                src = src.at[m] if len(src.shape) == 5 else src
                copy(src.at[pl.ds(2 * first, 2 * many)], dst.at[pl.ds(2 * (2 * n + first), 2 * many)])
    if edged:
        for m, dst in enumerate((kb, vb)):
            copy(edge.at[m, :, pl.ds(chunk * heads, heads)], dst.at[pl.ds(2 * EDGE, 2)])
    for c in copies[:len(sets)]:
        c.wait()
    for n in range(len(sets)):
        ints[pl.ds(8 * n, 8), :] = marks[n].astype(F32)[0:8].astype(jnp.int32)
    tables = pltpu.make_async_copy(ints, table, table_sem)
    tables.start()
    tables.wait()
    for c in copies[len(sets):]:
        c.wait()

    for n, (dh, window, far) in enumerate(sets):
        asker = height - dh
        there = (asker >= 0) & (asker < HA)

        def one_tile(tile, carry):
            frame, col = tile // 2, tile % 2
            count = jnp.int32(0)
            if window:
                for df in range(3):
                    near = 2 * shard + frame + df - 1
                    inside = there & (near >= 0) & (near < 2 * TA)
                    at = 2 * tx + frame + df - 1
                    piece = (at + 2 * SIDE) // 2 - tx
                    slot = 2 * (piece & (SIDE - 1)) + (at & 1)
                    slot = jnp.where((at < 0) | (at >= 2 * SIDE), EDGE, slot)
                    for kw in range(2):
                        number = df * 9 + (dh + 1) * 3 + (kw - col + 1)
                        used = (table[8 * n + tile, number] == 1) | ((dh == 0) & (number == 13))
                        listed[count] = slot * 2 + kw
                        count = count + (used & inside).astype(jnp.int32)
            if far:
                for j in range(SEL):
                    owner = table[8 * n + tile, CHOSEN + j]
                    piece = (owner + SIDE - tx) & (SIDE - 1)
                    listed[count] = (piece * 2 + frame) * 2 + col
                    count = count + (owner // SIDE == ty).astype(jnp.int32)
            listed[count] = listed[0]
            attend_tile(heads, tile, count, listed, q_bufs[n], kb, vb, outs[n], a_ref)
            return carry

        lax.fori_loop(0, 4, one_tile, 0)


def call_attend(heads, chunk, place, sets, queries, pieces, held, edge, earlier=(), together=False):
    anywhere = pl.BlockSpec(memory_space=pl.ANY)
    smem = pl.BlockSpec(memory_space=pltpu.SMEM)
    keys = pltpu.VMEM((18, heads, TILE, TILE), BF16)
    operands = list(queries)
    for piece, pair in zip(pieces, held):
        operands += list(pair) if piece else []
    operands += [] if edge is None else [edge]
    operands += list(earlier)
    count = 2 * len(sets) + 2 * sum(piece is not None for piece in pieces) + 2 * (edge is not None)
    rows = 4 * (heads * TILE + STAT)
    return pl.pallas_call(
        functools.partial(attend_kernel, heads, chunk, sets, pieces, edge is not None, len(earlier), together),
        out_shape=[jax.ShapeDtypeStruct((SIDE, rows, TILE), BF16)]
        if together
        else [jax.ShapeDtypeStruct((rows, TILE), BF16)] * len(sets),
        in_specs=[smem] + [anywhere] * len(operands),
        out_specs=[pl.BlockSpec(memory_space=pltpu.VMEM)] * (1 if together else len(sets)),
        scratch_shapes=[pltpu.VMEM((4, heads, TILE, TILE), BF16) for _ in sets]
        + [keys, keys, pltpu.VMEM((len(sets), TABLE, TILE), BF16)]
        + [pltpu.VMEM((8 * len(sets), TILE), jnp.int32), pltpu.SMEM((8 * len(sets), TILE), jnp.int32)]
        + [pltpu.SMEM((16,), jnp.int32), pltpu.VMEM((heads, TILE, TILE), F32)]
        + [pltpu.SemaphoreType.DMA((count,)), pltpu.SemaphoreType.DMA],
        compiler_params=pltpu.CompilerParams(vmem_limit_bytes=VMEM_LIMIT),
    )(place, *operands)


def arrange_kernel(heads, chosen, window, q_in, k_in, v_in, *refs):
    outs, (q, k, v, marks, sems) = refs[:-5], refs[-5:]
    q_out, both = outs[0], outs[1:]
    copies = [pltpu.make_async_copy(src, dst, sems.at[n]) for n, (src, dst) in enumerate(((k_in, k), (v_in, v), (q_in, q)))]
    for c in copies:
        c.start()
    marks[...] = jnp.zeros_like(marks)
    marks[pl.ds(0, 4), pl.ds(0, 27)] = window[...].astype(F32)
    marks[pl.ds(0, 4), pl.ds(CHOSEN, SEL)] = chosen[...].astype(F32)
    q_out[4, 0, pl.ds(0, TABLE)] = marks[...].astype(BF16)
    per = heads // CHUNKS
    tiles = [(tile, h, h // per, h % per, pl.ds(h * HEAD, HEAD)) for tile in range(4) for h in range(heads)]
    copies[0].wait()
    for tile, h, chunk, at, lanes in tiles:
        both[chunk][0, tile, at] = k[tile // 2, :, tile % 2, :, lanes].reshape(TILE, HEAD)
    copies[1].wait()
    for tile, h, chunk, at, lanes in tiles:
        both[chunk][1, tile, at] = v[tile // 2, :, tile % 2, :, lanes].reshape(TILE, HEAD).T
    copies[2].wait()
    for tile, h, chunk, at, lanes in tiles:
        q_out[tile, h] = q[tile // 2, :, tile % 2, :, lanes].reshape(TILE, HEAD)


def tie_kernel(*refs):
    del refs


def tie(arrays, earlier):
    anywhere = pl.BlockSpec(memory_space=pl.ANY)
    return pl.pallas_call(
        tie_kernel,
        out_shape=[jax.ShapeDtypeStruct(a.shape, a.dtype) for a in arrays],
        in_specs=[anywhere] * (len(arrays) + len(earlier)),
        out_specs=[anywhere] * len(arrays),
        input_output_aliases={n: n for n in range(len(arrays))},
    )(*arrays, *earlier)


def combine_kernel(heads, parts, place, *refs):
    sources, out = refs[:-1], refs[-1]
    height = place[2]
    there = {parts - 2: height > 0, parts - 1: height < HA - 1}
    for chunk in range(CHUNKS):
        mine = sources[chunk * 2 * parts:(chunk + 1) * 2 * parts]
        tokens, stats = mine[:parts], mine[parts:]
        logs = []
        for n in range(parts):
            s = stats[n][...].astype(F32)
            log = s[0:8] + s[8:16] + s[16:24]
            logs.append(jnp.where(there[n], log, NONE) if n in there else log)
        top = functools.reduce(jnp.maximum, logs)
        raised = [jnp.exp2(log - top) for log in logs]
        under = 1.0 / functools.reduce(jnp.add, raised)
        weights = [r * under for r in raised]
        for h in range(heads):
            terms = [weights[n][h:h + 1] * tokens[n][pl.ds(h * TILE, TILE), :].astype(F32) for n in range(parts)]
            mixed = functools.reduce(jnp.add, terms).T.astype(BF16)
            lanes = pl.ds((chunk * heads + h) * HEAD, HEAD)
            out[0, :, 0, :, lanes] = mixed.reshape(4, 32, HEAD)


def body(query, keys, values, selected, window_mask):
    frames, rows, cols, channels = query.shape
    heads = channels // HEAD // CHUNKS
    shard = lax.axis_index("ta")
    height = lax.axis_index("ha")
    tx, ty = shard % SIDE, shard // SIDE
    place = jnp.stack([tx, ty, height]).astype(jnp.int32)
    right, left, up, down = along_x(1), along_x(-1), along_y(1), along_y(-1)
    opposite = along_y(2)
    columns = [[SIDE * y + x for y in range(SIDE)] for x in range(SIDE)]
    ends = [(SIDE * y, SIDE * y + SIDE) for y in range(SIDE - 1)]
    ends = ends + [(SIDE * y + SIDE + 3, SIDE * y + 3) for y in range(SIDE - 1)]
    higher = [(i, i + 1) for i in range(HA - 1)]
    lower = [(b, a) for a, b in higher]

    def permute(array, pairs, axis="ta"):
        return lax.ppermute(array, axis, pairs)

    vmem, anywhere = [pl.BlockSpec(memory_space=m) for m in (pltpu.VMEM, pl.ANY)]
    blocks = [a.reshape(frames, rows, 2, 32, channels) for a in (query, keys, values)]
    q, *both = pl.pallas_call(
        functools.partial(arrange_kernel, heads * CHUNKS),
        out_shape=[jax.ShapeDtypeStruct((5, heads * CHUNKS, TILE, TILE), BF16)]
        + [jax.ShapeDtypeStruct((2, 4, heads, TILE, TILE), BF16)] * CHUNKS,
        in_specs=[vmem, vmem] + [anywhere] * 3,
        out_specs=[vmem] * (1 + CHUNKS),
        scratch_shapes=[pltpu.VMEM(blocks[0].shape, BF16) for _ in range(3)]
        + [pltpu.VMEM((TABLE, TILE), F32), pltpu.SemaphoreType.DMA((3,))],
        compiler_params=pltpu.CompilerParams(vmem_limit_bytes=VMEM_LIMIT),
    )(selected.reshape(4, SEL), window_mask.reshape(4, 27), *blocks)

    q1, q2, q3 = permute(q, up), permute(q, opposite), permute(q, down)
    (q,) = tie((q,), (q1, q3))
    q_low, q_high = permute(q, higher, "ha"), permute(q, lower, "ha")
    from_left, from_right = [], []
    for c in range(CHUNKS):
        if c:
            (both[c],) = tie((both[c],), (from_left[-1], from_right[-1]))
        from_left.append(permute(both[c], right))
        from_right.append(permute(both[c], left))
    far_k = [permute(b[0], right) for b in from_left]
    far_v = [permute(b[1], left) for b in from_right]
    edge = [jnp.where(tx == 0, a[:, 2:], b[:, :2]) for a, b in zip(from_left, from_right)]
    edge = permute(jnp.concatenate(edge, 2), ends)

    partial = []
    whole = ((0, 2),) * SIDE
    for c in range(CHUNKS):
        held = ((both[c],) * 2, (from_right[c],) * 2, (far_k[c], far_v[c]), (from_left[c],) * 2)
        far_sets = ((0, False, True),) * SIDE
        (parts,) = call_attend(heads, c, place, far_sets, (q, q1, q2, q3), whole, held, None, (edge, q_low, q_high), True)
        arrived = lax.all_to_all(parts, "ta", 0, 0, axis_index_groups=columns, tiled=True)
        near = ((0, 2), (0, 1), None, (1, 1))
        for_low, for_high = call_attend(
            heads, c, place, ((1, True, False), (-1, True, False)), (q_low, q_high), near, held, edge, (parts,)
        )
        from_high, from_low = permute(for_low, lower, "ha"), permute(for_high, higher, "ha")
        (mine,) = call_attend(heads, c, place, ((0, True, False),), (q,), near, held, edge, (for_low,))
        partial.append([arrived] * SIDE + [mine, from_low, from_high])

    count = len(partial[0])
    tokens, stats = [], []
    for n in range(count):
        lead, at = ((None,), (n,)) if n < SIDE else ((), ())
        tokens.append(pl.BlockSpec(lead + (heads * TILE, TILE), lambda t, at=at: at + (t, 0)))
        stats.append(pl.BlockSpec(lead + (STAT, TILE), lambda t, at=at: at + (4 * heads * TILE // STAT + t, 0)))
    out = pl.pallas_call(
        functools.partial(combine_kernel, heads, count),
        out_shape=jax.ShapeDtypeStruct((frames, rows, 2, 32, channels), BF16),
        grid=(4,),
        in_specs=[pl.BlockSpec(memory_space=pltpu.SMEM)] + (tokens + stats) * CHUNKS,
        out_specs=pl.BlockSpec((1, rows, 1, 32, channels), lambda t: (t // 2, 0, t % 2, 0, 0)),
        compiler_params=pltpu.CompilerParams(vmem_limit_bytes=VMEM_LIMIT),
    )(place, *[a for some in partial for a in some + some])
    return out.reshape(frames, rows, cols, channels)


def solution(mesh):
    block = P("ta", "ha", None, "hd")
    table = P("ta", "ha", None, None)
    return jax.shard_map(
        body, mesh=mesh, in_specs=(block, block, block, table, table), out_specs=block, check_vma=False
    )
```

```python
import functools
import jax
import jax.numpy as jnp
import numpy as np
from jax import lax
from jax.experimental import pallas as pl
from jax.experimental.pallas import tpu as pltpu
from jax.sharding import PartitionSpec as P

HEAD = 128
TILE = 128
SEL = 4
SIDE = 4
TA = SIDE * SIDE
HA = 8
STAT = 32
TABLE = 16
CHOSEN = 32
EDGE = 8
CHUNKS = 1
NONE = -1e30
SCALE = float(HEAD ** -0.5)
LOG2E = float(np.log2(np.e))
VMEM_LIMIT = 60 * 1024 * 1024
F32 = jnp.float32
BF16 = jnp.bfloat16


def along_x(step):
    return [(SIDE * y + x, SIDE * y + (x + step) % SIDE) for y in range(SIDE) for x in range(SIDE)]


def along_y(step):
    return [(SIDE * y + x, SIDE * ((y + step) % SIDE) + x) for y in range(SIDE) for x in range(SIDE)]


def attend_tile(heads, tile, count, listed, q_ref, k_ref, v_ref, o_ref, a_ref):
    stat_rows = pl.ds(pl.multiple_of((4 * heads) * TILE + STAT * tile, STAT), STAT)

    def out_rows(h):
        return pl.ds(pl.multiple_of((tile * heads + h) * TILE, TILE), TILE)

    def score(h, keys):
        q = q_ref[tile, h]
        return lax.dot_general(keys, q, (((1,), (1,)), ((), ())), preferred_element_type=F32) * (SCALE * LOG2E)

    def pair(i, h):
        a, b = listed[2 * i], listed[2 * i + 1]
        s = score(h, jnp.concatenate([k_ref[a, h], k_ref[b, h]], 0))
        s = jnp.concatenate([s[:TILE], jnp.where(2 * i + 1 < count, s[TILE:], NONE)], 0)
        return s, jnp.concatenate([v_ref[a, h], v_ref[b, h]], 1)

    def mix(values, p):
        return jnp.dot(values, p.astype(BF16), preferred_element_type=F32)

    def write(results):
        row = lax.broadcasted_iota(jnp.int32, (8, TILE), 0)
        stats = jnp.zeros((8, TILE), F32)
        for h, (top, total, mixed) in enumerate(results):
            o_ref[out_rows(h), :] = (mixed * (1.0 / total)).astype(BF16)
            stats = jnp.where(row == h, top + jnp.log2(total), stats)
        high = stats.astype(BF16).astype(F32)
        mid = (stats - high).astype(BF16).astype(F32)
        parts = jnp.concatenate([high, mid, stats - high - mid, jnp.zeros_like(stats)], 0)
        o_ref[stat_rows, :] = parts.astype(BF16)

    def once(scores):
        results = []
        for s, v in scores:
            top = jnp.max(s, axis=0, keepdims=True)
            p = jnp.exp2(s - top)
            results.append((top, jnp.sum(p, axis=0, keepdims=True), mix(v, p)))
        write(results)

    @pl.when(count == 0)
    def _():
        for h in range(heads):
            o_ref[out_rows(h), :] = jnp.zeros((TILE, TILE), BF16)
        row = lax.broadcasted_iota(jnp.int32, (STAT, TILE), 0)
        o_ref[stat_rows, :] = jnp.where(row < 8, NONE, 0.0).astype(BF16)

    @pl.when(count == 1)
    def _():
        once([(score(h, k_ref[listed[0], h]), v_ref[listed[0], h]) for h in range(heads)])

    @pl.when(count == 2)
    def _():
        once([pair(0, h) for h in range(heads)])

    @pl.when(count > 2)
    def _():
        for h in range(heads):
            a_ref[h] = jnp.zeros((TILE, TILE), F32)

        def step(i, carry):
            after = []
            for h in range(heads):
                top, total = carry[h]
                s, v = pair(i, h)
                higher = jnp.maximum(top, jnp.max(s, axis=0, keepdims=True))
                fade = jnp.exp2(top - higher)
                p = jnp.exp2(s - higher)
                a_ref[h] = a_ref[h] * fade + mix(v, p)
                after.append((higher, total * fade + jnp.sum(p, axis=0, keepdims=True)))
            return tuple(after)

        start = ((jnp.full((1, TILE), NONE, F32), jnp.zeros((1, TILE), F32)),) * heads
        ends = lax.fori_loop(0, (count + 1) // 2, step, start)
        write([(top, total, a_ref[h]) for h, (top, total) in enumerate(ends)])


def attend_kernel(heads, chunk, sets, pieces, edged, earlier, place, *refs):
    refs = list(refs)
    queries = [refs.pop(0) for _ in sets]
    held = [[refs.pop(0), refs.pop(0)] if piece else None for piece in pieces]
    edge = refs.pop(0) if edged else None
    del refs[:earlier]
    outs = [refs.pop(0) for _ in sets]
    q_bufs = [refs.pop(0) for _ in sets]
    kb, vb, marks, ints, table, listed, a_ref, sems, table_sem = refs
    tx, ty, height = place[0], place[1], place[2]
    shard = ty * SIDE + tx
    copies = []

    def copy(src, dst):
        c = pltpu.make_async_copy(src, dst, sems.at[len(copies)])
        c.start()
        copies.append(c)

    for n, (src, dst) in enumerate(zip(queries, q_bufs)):
        copy(src.at[4, 0, pl.ds(0, TABLE)], marks.at[n])
    for src, dst in zip(queries, q_bufs):
        copy(src.at[pl.ds(0, 4), pl.ds(chunk * heads, heads)], dst)
    for n, piece in enumerate(pieces):
        if piece:
            first, many = piece
            for m, dst in enumerate((kb, vb)):
                src = held[n][m]
                src = src.at[m] if len(src.shape) == 5 else src
                copy(src.at[pl.ds(2 * first, 2 * many)], dst.at[pl.ds(2 * (2 * n + first), 2 * many)])
    if edged:
        for m, dst in enumerate((kb, vb)):
            copy(edge.at[m, :, pl.ds(chunk * heads, heads)], dst.at[pl.ds(2 * EDGE, 2)])
    for c in copies[:len(sets)]:
        c.wait()
    for n in range(len(sets)):
        ints[pl.ds(8 * n, 8), :] = marks[n].astype(F32)[0:8].astype(jnp.int32)
    tables = pltpu.make_async_copy(ints, table, table_sem)
    tables.start()
    tables.wait()
    for c in copies[len(sets):]:
        c.wait()

    for n, (dh, window, far) in enumerate(sets):
        asker = height - dh
        there = (asker >= 0) & (asker < HA)

        def one_tile(tile, carry):
            frame, col = tile // 2, tile % 2
            count = jnp.int32(0)
            if window:
                for df in range(3):
                    near = 2 * shard + frame + df - 1
                    inside = there & (near >= 0) & (near < 2 * TA)
                    at = 2 * tx + frame + df - 1
                    piece = (at + 2 * SIDE) // 2 - tx
                    slot = 2 * (piece & (SIDE - 1)) + (at & 1)
                    slot = jnp.where((at < 0) | (at >= 2 * SIDE), EDGE, slot)
                    for kw in range(2):
                        number = df * 9 + (dh + 1) * 3 + (kw - col + 1)
                        used = (table[8 * n + tile, number] == 1) | ((dh == 0) & (number == 13))
                        listed[count] = slot * 2 + kw
                        count = count + (used & inside).astype(jnp.int32)
            if far:
                for j in range(SEL):
                    owner = table[8 * n + tile, CHOSEN + j]
                    piece = (owner + SIDE - tx) & (SIDE - 1)
                    listed[count] = (piece * 2 + frame) * 2 + col
                    count = count + (owner // SIDE == ty).astype(jnp.int32)
            listed[count] = listed[0]
            attend_tile(heads, tile, count, listed, q_bufs[n], kb, vb, outs[n], a_ref)
            return carry

        lax.fori_loop(0, 4, one_tile, 0)


def call_attend(heads, chunk, place, sets, queries, pieces, held, edge, earlier=()):
    anywhere = pl.BlockSpec(memory_space=pl.ANY)
    smem = pl.BlockSpec(memory_space=pltpu.SMEM)
    keys = pltpu.VMEM((18, heads, TILE, TILE), BF16)
    operands = list(queries)
    for piece, pair in zip(pieces, held):
        operands += list(pair) if piece else []
    operands += [] if edge is None else [edge]
    operands += list(earlier)
    count = 2 * len(sets) + 2 * sum(piece is not None for piece in pieces) + 2 * (edge is not None)
    rows = 4 * (heads * TILE + STAT)
    return pl.pallas_call(
        functools.partial(attend_kernel, heads, chunk, sets, pieces, edge is not None, len(earlier)),
        out_shape=[jax.ShapeDtypeStruct((rows, TILE), BF16)] * len(sets),
        in_specs=[smem] + [anywhere] * len(operands),
        out_specs=[pl.BlockSpec(memory_space=pltpu.VMEM)] * len(sets),
        scratch_shapes=[pltpu.VMEM((4, heads, TILE, TILE), BF16) for _ in sets]
        + [keys, keys, pltpu.VMEM((len(sets), TABLE, TILE), BF16)]
        + [pltpu.VMEM((8 * len(sets), TILE), jnp.int32), pltpu.SMEM((8 * len(sets), TILE), jnp.int32)]
        + [pltpu.SMEM((16,), jnp.int32), pltpu.VMEM((heads, TILE, TILE), F32)]
        + [pltpu.SemaphoreType.DMA((count,)), pltpu.SemaphoreType.DMA],
        compiler_params=pltpu.CompilerParams(vmem_limit_bytes=VMEM_LIMIT),
    )(place, *operands)


def arrange_kernel(heads, place, chosen, window, q_in, k_in, v_in, *refs):
    outs, (q, k, v, marks, sems) = refs[:-5], refs[-5:]
    q_out, edge, both = outs[0], outs[1], outs[2:]
    copies = [pltpu.make_async_copy(src, dst, sems.at[n]) for n, (src, dst) in enumerate(((k_in, k), (v_in, v), (q_in, q)))]
    for c in copies:
        c.start()
    marks[...] = jnp.zeros_like(marks)
    marks[pl.ds(0, 4), pl.ds(0, 27)] = window[...].astype(F32)
    marks[pl.ds(0, 4), pl.ds(CHOSEN, SEL)] = chosen[...].astype(F32)
    q_out[4, 0, pl.ds(0, TABLE)] = marks[...].astype(BF16)
    per = heads // CHUNKS
    tiles = [(tile, h, h // per, h % per, pl.ds(h * HEAD, HEAD)) for tile in range(4) for h in range(heads)]
    copies[0].wait()
    for tile, h, chunk, at, lanes in tiles:
        both[chunk][0, tile, at] = k[tile // 2, :, tile % 2, :, lanes].reshape(TILE, HEAD)
    copies[1].wait()
    for tile, h, chunk, at, lanes in tiles:
        both[chunk][1, tile, at] = v[tile // 2, :, tile % 2, :, lanes].reshape(TILE, HEAD).T
    copies[2].wait()
    for tile, h, chunk, at, lanes in tiles:
        q_out[tile, h] = q[tile // 2, :, tile % 2, :, lanes].reshape(TILE, HEAD)
    first = jnp.where(place[0] == 0, 0, 2)
    for chunk in range(CHUNKS):
        for n in range(2):
            for col in range(2):
                edge[n, col, pl.ds(chunk * per, per)] = both[chunk][n, first + col]


def tie_kernel(*refs):
    del refs


def tie(arrays, earlier):
    anywhere = pl.BlockSpec(memory_space=pl.ANY)
    return pl.pallas_call(
        tie_kernel,
        out_shape=[jax.ShapeDtypeStruct(a.shape, a.dtype) for a in arrays],
        in_specs=[anywhere] * (len(arrays) + len(earlier)),
        out_specs=[anywhere] * len(arrays),
        input_output_aliases={n: n for n in range(len(arrays))},
    )(*arrays, *earlier)


def combine_kernel(heads, parts, place, *refs):
    sources, out = refs[:-1], refs[-1]
    height = place[2]
    there = {parts - 2: height > 0, parts - 1: height < HA - 1}
    for chunk in range(CHUNKS):
        mine = sources[chunk * 2 * parts:(chunk + 1) * 2 * parts]
        tokens, stats = mine[:parts], mine[parts:]
        logs = []
        for n in range(parts):
            s = stats[n][...].astype(F32)
            log = s[0:8] + s[8:16] + s[16:24]
            logs.append(jnp.where(there[n], log, NONE) if n in there else log)
        top = functools.reduce(jnp.maximum, logs)
        raised = [jnp.exp2(log - top) for log in logs]
        under = 1.0 / functools.reduce(jnp.add, raised)
        weights = [r * under for r in raised]
        for h in range(heads):
            terms = [weights[n][h:h + 1] * tokens[n][pl.ds(h * TILE, TILE), :].astype(F32) for n in range(parts)]
            mixed = functools.reduce(jnp.add, terms).T.astype(BF16)
            lanes = pl.ds((chunk * heads + h) * HEAD, HEAD)
            out[0, :, 0, :, lanes] = mixed.reshape(4, 32, HEAD)


def body(query, keys, values, selected, window_mask):
    frames, rows, cols, channels = query.shape
    heads = channels // HEAD // CHUNKS
    shard = lax.axis_index("ta")
    height = lax.axis_index("ha")
    tx, ty = shard % SIDE, shard // SIDE
    place = jnp.stack([tx, ty, height]).astype(jnp.int32)
    right, left, up, down = along_x(1), along_x(-1), along_y(1), along_y(-1)
    opposite = along_y(2)
    ends = [(SIDE * y + 3, SIDE * y + 4) for y in range(SIDE - 1)]
    ends = ends + [(b, a) for a, b in ends]
    higher = [(i, i + 1) for i in range(HA - 1)]
    lower = [(b, a) for a, b in higher]

    def permute(array, pairs, axis="ta"):
        return lax.ppermute(array, axis, pairs)

    smem, vmem, anywhere = [pl.BlockSpec(memory_space=m) for m in (pltpu.SMEM, pltpu.VMEM, pl.ANY)]
    blocks = [a.reshape(frames, rows, 2, 32, channels) for a in (query, keys, values)]
    q, edge, *both = pl.pallas_call(
        functools.partial(arrange_kernel, heads * CHUNKS),
        out_shape=[jax.ShapeDtypeStruct((5, heads * CHUNKS, TILE, TILE), BF16)]
        + [jax.ShapeDtypeStruct((2, 2, heads * CHUNKS, TILE, TILE), BF16)]
        + [jax.ShapeDtypeStruct((2, 4, heads, TILE, TILE), BF16)] * CHUNKS,
        in_specs=[smem, vmem, vmem] + [anywhere] * 3,
        out_specs=[vmem] * (2 + CHUNKS),
        scratch_shapes=[pltpu.VMEM(blocks[0].shape, BF16) for _ in range(3)]
        + [pltpu.VMEM((TABLE, TILE), F32), pltpu.SemaphoreType.DMA((3,))],
        compiler_params=pltpu.CompilerParams(vmem_limit_bytes=VMEM_LIMIT),
    )(place, selected.reshape(4, SEL), window_mask.reshape(4, 27), *blocks)

    q_low, q_high = permute(q, higher, "ha"), permute(q, lower, "ha")
    q2 = permute(q, opposite)
    q, edge = tie((q, edge), (q2, q_low, q_high))
    q1, q3 = permute(q, up), permute(q, down)
    edge = permute(edge, ends)
    from_left, from_right = [], []
    for c in range(CHUNKS):
        if c:
            (both[c],) = tie((both[c],), (from_left[-1], from_right[-1]))
        from_left.append(permute(both[c], right))
        from_right.append(permute(both[c], left))
    far_k = [permute(b[0], right) for b in from_left]
    far_v = [permute(b[1], left) for b in from_right]

    partial = []
    whole = ((0, 2),) * SIDE
    for c in range(CHUNKS):
        held = ((both[c],) * 2, (from_right[c],) * 2, (far_k[c], far_v[c]), (from_left[c],) * 2)
        for_low, for_high = call_attend(
            heads, c, place, ((1, True, False), (-1, True, False)), (q_low, q_high),
            ((0, 2), (0, 1), None, (1, 1)), held, edge,
        )
        o1, o2, o3 = call_attend(heads, c, place, ((0, False, True),) * 3, (q1, q2, q3), whole, held, None)
        f2, f1, f3 = permute(o2, opposite), permute(o1, down), permute(o3, up)
        for_low, for_high = tie((for_low, for_high), (o1,))
        from_high, from_low = permute(for_low, lower, "ha"), permute(for_high, higher, "ha")
        (mine,) = call_attend(heads, c, place, ((0, True, True),), (q,), whole, held, edge, (o1,))
        partial.append([mine, f1, f2, f3, from_low, from_high])

    count = len(partial[0])
    token_spec = pl.BlockSpec((heads * TILE, TILE), lambda t: (t, 0))
    stat_spec = pl.BlockSpec((STAT, TILE), lambda t: (4 * heads * TILE // STAT + t, 0))
    out = pl.pallas_call(
        functools.partial(combine_kernel, heads, count),
        out_shape=jax.ShapeDtypeStruct((frames, rows, 2, 32, channels), BF16),
        grid=(4,),
        in_specs=[pl.BlockSpec(memory_space=pltpu.SMEM)] + ([token_spec] * count + [stat_spec] * count) * CHUNKS,
        out_specs=pl.BlockSpec((1, rows, 1, 32, channels), lambda t: (t // 2, 0, t % 2, 0, 0)),
        compiler_params=pltpu.CompilerParams(vmem_limit_bytes=VMEM_LIMIT),
    )(place, *[a for some in partial for a in some + some])
    return out.reshape(frames, rows, cols, channels)


def solution(mesh):
    block = P("ta", "ha", None, "hd")
    table = P("ta", "ha", None, None)
    return jax.shard_map(
        body, mesh=mesh, in_specs=(block, block, block, table, table), out_specs=block, check_vma=False
    )
```
